32 devices in a mesh: parts: 2 (over y), dp: 4 (over z), tensor: 4 (over x, core).
Axes of the slice: x: 2, y: 2, z: 4, core: 2. Of those that a mesh axis runs over, the one named last changes fastest.
Arguments:
- queries: bfloat16 [4096, 8192], P(('parts', 'dp'), 'tensor'), parts along dimension 0, may hold values from -128 to 128
- prefix_key_cache: bfloat16 [2048, 1024], P('parts', 'tensor'), parts along dimension 0, may hold values from -8 to 8
- prefix_value_cache: bfloat16 [2048, 1024], P('parts', 'tensor'), parts along dimension 0, may hold values from -6 to 6
- prompt_keys: bfloat16 [4096, 1024], P(('parts', 'dp'), 'tensor'), parts along dimension 0, may hold values from -6 to 6
- prompt_values: bfloat16 [4096, 1024], P(('parts', 'dp'), 'tensor'), parts along dimension 0, may hold values from -6 to 6
- output_weight: bfloat16 [8192, 4096], P('tensor', 'dp'), may hold values from -1 to 1
- adapter_down_weight: bfloat16 [64, 16, 8192], P(('parts', 'dp'), None, 'tensor'), parts along dimension 0, may hold values from -1 to 1
- adapter_up_weight: bfloat16 [64, 16, 4096], P(('parts', 'dp'), None, 'tensor'), parts along dimension 0, may hold values from -1.5 to 1.5
- adapter_row_map: int32 [64], P('parts'), parts along dimension 0, may hold values from 0 to 31, as said below
- prompt_adapter: int32 [16], P('parts'), parts along dimension 0, may hold values from 0 to 31, as said below
- prompt_length: int32 [16], P('parts'), parts along dimension 0, may hold values from 1 to 256, as said below
- prefix_read_length: int32 [16], P('parts'), parts along dimension 0, may hold values from 2 to 1024, as said below
Outputs:
- projected: bfloat16 [4096, 4096], P(('parts', 'dp'), 'tensor'), parts along dimension 0
The draws below stay inside these ranges and needn't reach their ends.
There are 2 independent parts, one for each index of `parts`. The reference program is written for one: setup_inputs(seed, part) draws one part's arguments, and reference() takes and returns one part's arrays. A program takes and returns all parts, laid end to end along the dimension named above; an argument that names none is the same for every part. Nothing has to cross between parts.
Inputs may be any that keep to these rules, and one draw needn't show every extreme that they name: `adapter_row_map`: a permutation. `prompt_adapter`: among the 2 prompts of one dp group (prompts g * 2 to g * 2 + 1) at most 1 use adapters whose stored rows lie in one and the same group along dp; in every draw some one group stores the adapters of 1 prompts of every dp group. `prompt_length`: some prompt in each draw is full. `prefix_read_length`: some prompt in each draw reads the whole cache.
All inputs are finite; a program needn't handle non-finite values.
Results may differ from the reference program's by a relative error of at most 0.009.
Values may be sent and summed in bfloat16 or wider, within the bound.
A program may use at most 128 MiB of HBM per device.

```python
import jax
import jax.numpy as jnp
from jax import lax

HEADS = 64
KVH = 8
HD = 128
QUERY_FEATURES = 8192
KVD = 1024
OUTPUT_FEATURES = 4096
ADAPTER_RANK = 16
ADAPT_DEV = 8
NSEG = 2
CAP = 1
P_SIZE = 1024
SEG = 256
TOKEN_SLOTS = 2048
SEGS = 8
ADAPTER_TOTAL = 32
N_DP = 4


def cache_base(key):
    return jnp.clip(jax.random.normal(jax.random.fold_in(key, 101), (P_SIZE, KVD), jnp.float32), -4.0, 4.0)


def adapter_table(key):
    return jax.random.permutation(jax.random.fold_in(key, 11), N_DP * ADAPT_DEV).astype(jnp.int32)


def draw_prefix_key_cache(key, part):
    base_output = cache_base(key)
    return base_output.astype(jnp.bfloat16)


def draw_queries(key, part):
    own_key = jax.random.fold_in(key, 7)
    drawn = jnp.clip(jax.random.normal(own_key, (TOKEN_SLOTS, QUERY_FEATURES), jnp.float32), -6.0, 6.0)
    return drawn.astype(jnp.bfloat16)


def draw_adapter_row_map(key, part):
    return adapter_table(key)


def draw_prompt_adapter(key, part):
    table = adapter_table(key)
    inverse = jnp.argsort(table, stable=True).astype(jnp.int32)
    key = jax.random.fold_in(key, 13)
    first_key, second_key, third_key = jax.random.split(key, 3)
    special = jax.random.randint(first_key, (), 0, N_DP)

    def group_owners(group_key):
        left_key, right_key = jax.random.split(group_key)
        others = (special + 1 + jax.random.permutation(left_key, N_DP - 1)[:NSEG - CAP]) % N_DP
        owners = jnp.concatenate([jnp.full((CAP,), special, jnp.int32), others.astype(jnp.int32)])
        return owners[jax.random.permutation(right_key, NSEG)]
    owners = jax.vmap(group_owners)(jax.random.split(second_key, N_DP)).reshape(-1)
    within = jax.random.randint(third_key, (N_DP * NSEG,), 0, ADAPT_DEV)
    return inverse[owners * ADAPT_DEV + within].astype(jnp.int32)


def draw_prompt_length(key, part):
    key = jax.random.fold_in(key, 17)
    left_key, right_key = jax.random.split(key)
    lengths = jax.random.randint(left_key, (N_DP * NSEG,), 1, SEG + 1)
    where_full = jax.random.randint(right_key, (), 0, N_DP * NSEG)
    return lengths.at[where_full].set(SEG).astype(jnp.int32)


def draw_prefix_read_length(key, part):
    key = jax.random.fold_in(key, 19)
    left_key, right_key = jax.random.split(key)
    lengths = jax.random.randint(left_key, (N_DP * NSEG,), 2, P_SIZE + 1)
    where_full = jax.random.randint(right_key, (), 0, N_DP * NSEG)
    return lengths.at[where_full].set(P_SIZE).astype(jnp.int32)


def level_of(rng, extent, cuts, low, top_value):
    level = 1.0
    for axis_at, blocks in cuts:
        steps = jax.random.uniform(jax.random.fold_in(jax.random.fold_in(rng, 6), axis_at), (blocks,), jnp.float32, low / len(cuts), top_value / len(cuts))
        level = level * jnp.repeat(jnp.exp(steps), extent[axis_at] // blocks).reshape((-1,) + (1,) * (len(extent) - 1 - axis_at))
    return level


def normal_values(key, dims, spread, bound, pieces=(), kind=jnp.bfloat16):
    result = jax.random.normal(key, dims, jnp.float32) * spread
    if len(pieces) > 0:
        result = level_of(key, dims, pieces, -0.22, 0.18) * result
    return jnp.clip(result, min=-bound, max=bound).astype(kind)


def setup_inputs(seed: int = 0, part: int = 0) -> dict:
    splits = jax.random.split(jax.random.key(seed), 13)
    part_splits = jax.random.split(jax.random.fold_in(splits[12], part), 13)
    return {
        "queries": draw_queries(jax.random.fold_in(jax.random.fold_in(splits[12], part), 71), part),
        "prefix_key_cache": draw_prefix_key_cache(jax.random.fold_in(jax.random.fold_in(splits[12], part), 71), part),
        "prefix_value_cache": normal_values(part_splits[2], (P_SIZE, KVD), 1.0, 6.0, ((1, 4),)),
        "prompt_keys": normal_values(part_splits[3], (TOKEN_SLOTS, KVD), 1.0, 6.0, ((0, 4), (1, 4))),
        "prompt_values": normal_values(part_splits[4], (TOKEN_SLOTS, KVD), 1.0, 6.0, ((0, 4), (1, 4))),
        "output_weight": normal_values(splits[5], (QUERY_FEATURES, OUTPUT_FEATURES), (max(QUERY_FEATURES // 256, 1)) ** -0.5, 1.0, ((0, 4), (1, 4))),
        "adapter_down_weight": normal_values(part_splits[6], (ADAPTER_TOTAL, ADAPTER_RANK, QUERY_FEATURES), (max(QUERY_FEATURES // 256, 1)) ** -0.5, 1.0, ((0, 4), (2, 4))),
        "adapter_up_weight": normal_values(part_splits[7], (ADAPTER_TOTAL, ADAPTER_RANK, OUTPUT_FEATURES), ADAPTER_RANK ** -0.5, 1.5, ((0, 4), (2, 4))),
        "adapter_row_map": draw_adapter_row_map(jax.random.fold_in(jax.random.fold_in(splits[12], part), 71), part),
        "prompt_adapter": draw_prompt_adapter(jax.random.fold_in(jax.random.fold_in(splits[12], part), 71), part),
        "prompt_length": draw_prompt_length(jax.random.fold_in(jax.random.fold_in(splits[12], part), 71), part),
        "prefix_read_length": draw_prefix_read_length(jax.random.fold_in(jax.random.fold_in(splits[12], part), 71), part),
    }


adapter_scale = 2.0


def attend(query_rows, own_keys, own_values, prefix_key_cache, prefix_value_cache, prefix_count):
    group_size = HEADS // KVH
    scale = HD ** -0.5
    query_four = query_rows.reshape(SEG, KVH, group_size, HD).astype(jnp.float32)
    cache_keys = prefix_key_cache.reshape(P_SIZE, KVH, HD).astype(jnp.float32)
    cache_values = prefix_value_cache.reshape(P_SIZE, KVH, HD).astype(jnp.float32)
    own_key_heads = own_keys.reshape(SEG, KVH, HD).astype(jnp.float32)
    own_value_heads = own_values.reshape(SEG, KVH, HD).astype(jnp.float32)
    scores = jnp.einsum('skgd,pkd->skgp', query_four, cache_keys) * scale
    own_score = jnp.einsum('skgd,skd->skg', query_four, own_key_heads) * scale
    valid = jnp.arange(P_SIZE, dtype=jnp.int32) < prefix_count
    scores = jnp.where(valid, scores, -jnp.inf)
    highest = jnp.maximum(jnp.max(scores, axis=-1), own_score)
    expon = jnp.exp(scores - highest[..., None])
    own_expon = jnp.exp(own_score - highest)
    total = jnp.sum(expon, axis=-1) + own_expon
    weights = (expon / total[..., None]).astype(jnp.bfloat16)
    own_weight = (own_expon / total).astype(jnp.bfloat16)
    context = jnp.einsum('skgp,pkd->skgd', weights.astype(jnp.float32), cache_values)
    context = context + own_weight.astype(jnp.float32)[..., None] * own_value_heads[:, :, None, :]
    return context.reshape(SEG, QUERY_FEATURES).astype(jnp.bfloat16)


def reference(queries, prefix_key_cache, prefix_value_cache, prompt_keys, prompt_values, output_weight, adapter_down_weight, adapter_up_weight, adapter_row_map, prompt_adapter, prompt_length, prefix_read_length):
    def one_prompt(prompt):
        begin = (prompt * SEG).astype(jnp.int32)
        query_rows = lax.dynamic_slice_in_dim(queries, begin, SEG, 0)
        own_keys = lax.dynamic_slice_in_dim(prompt_keys, begin, SEG, 0)
        own_values = lax.dynamic_slice_in_dim(prompt_values, begin, SEG, 0)
        context = attend(query_rows, own_keys, own_values, prefix_key_cache, prefix_value_cache, prefix_read_length[prompt])
        live = (jnp.arange(SEG, dtype=jnp.int32) < prompt_length[prompt]).astype(jnp.bfloat16)
        return context * live[:, None]

    context = lax.map(one_prompt, jnp.arange(SEGS, dtype=jnp.int32))
    base_output = jnp.dot(context.reshape(TOKEN_SLOTS, QUERY_FEATURES), output_weight, preferred_element_type=jnp.float32)
    stored_row = adapter_row_map[prompt_adapter].astype(jnp.int32)
    down_matrix_rows = adapter_down_weight[stored_row]
    up_matrix_rows = adapter_up_weight[stored_row]
    lowrank = jnp.einsum('sxf,srf->sxr', context.astype(jnp.float32), down_matrix_rows.astype(jnp.float32)).astype(jnp.bfloat16)
    adapter_delta = jnp.einsum('sxr,sro->sxo', lowrank.astype(jnp.float32), up_matrix_rows.astype(jnp.float32)).astype(jnp.bfloat16)
    projected = base_output + adapter_scale * adapter_delta.reshape(TOKEN_SLOTS, OUTPUT_FEATURES).astype(jnp.float32)
    return projected.astype(jnp.bfloat16)
```

```python
import jax
import jax.numpy as jnp
from jax import lax
from jax.sharding import PartitionSpec as P

HD = 128
CAP = 1
PIECES = 2


adapter_scale = 2.0


def rank_total(partial_value):
    return lax.psum(partial_value, "tensor")


def local_attention(
    queries, prefix_key_cache, prefix_value_cache, prompt_keys, prompt_values, token_prefix
):
    tok_rows, query_width = queries.shape
    positions, key_width = prefix_key_cache.shape
    local_kv = key_width // HD
    group_size = query_width // key_width
    scale = HD ** (-0.5)
    query_four = queries.reshape(tok_rows, local_kv, group_size, HD)
    cache_keys = prefix_key_cache.reshape(positions, local_kv, HD)
    cache_values = prefix_value_cache.reshape(positions, local_kv, HD)
    own_key_heads = prompt_keys.reshape(tok_rows, local_kv, HD)
    own_value_heads = prompt_values.reshape(tok_rows, local_kv, HD)
    scores = (
        jnp.einsum("tkgd,pkd->kgtp", query_four, cache_keys, preferred_element_type=jnp.float32)
        * scale
    )
    own_score = (
        jnp.einsum("tkgd,tkd->kgt", query_four, own_key_heads, preferred_element_type=jnp.float32)
        * scale
    )
    valid = jnp.arange(positions, dtype=jnp.int32)[None, :] < token_prefix[:, None]
    scores = jnp.where(valid[None, None], scores, -jnp.inf)
    highest = jnp.maximum(jnp.max(scores, axis=-1), own_score)
    expon = jnp.exp(scores - highest[..., None])
    own_expon = jnp.exp(own_score - highest)
    total = jnp.sum(expon, axis=-1) + own_expon
    weights = (expon / total[..., None]).astype(jnp.bfloat16)
    own_weight = (own_expon / total).astype(jnp.bfloat16)
    context = jnp.einsum(
        "kgtp,pkd->tkgd", weights, cache_values, preferred_element_type=jnp.float32
    )
    context = context + jnp.einsum(
        "kgt,tkd->tkgd", own_weight, own_value_heads, preferred_element_type=jnp.float32
    )
    return context.reshape(tok_rows, query_width).astype(jnp.bfloat16)


def selected_blocks(local_adapter_index, adapter_down_weight, adapter_up_weight):
    adapter_number = adapter_down_weight.shape[0]
    adapter_selector = (
        local_adapter_index[..., None] == jnp.arange(adapter_number, dtype=jnp.int32)
    ).astype(jnp.bfloat16)
    down_selected = jnp.einsum(
        "ljm,mes->ljes", adapter_selector, adapter_down_weight, preferred_element_type=jnp.float32
    ).astype(jnp.bfloat16)
    up_selected = jnp.einsum(
        "yuv,vzj->yuzj", adapter_selector, adapter_up_weight, preferred_element_type=jnp.float32
    ).astype(jnp.bfloat16)
    return (down_selected, up_selected)


def local(
    queries,
    prefix_key_cache,
    prefix_value_cache,
    prompt_keys,
    prompt_values,
    output_weight,
    adapter_down_weight,
    adapter_up_weight,
    adapter_row_map,
    prompt_adapter,
    prompt_length,
    prefix_read_length,
):
    group_count = lax.axis_size("dp")
    group = lax.axis_index("dp")
    tok_rows, query_width = queries.shape
    part_count = lax.axis_size("parts")
    half_rows = query_width // part_count
    piece_width = output_weight.shape[1] // PIECES
    half_weight = lax.dynamic_slice_in_dim(
        output_weight, lax.axis_index("parts") * half_rows, half_rows, axis=0
    )
    gathered_weights = [
        lax.all_gather(
            half_weight[:, piece * piece_width : (piece + 1) * piece_width], ("dp", "parts"), axis=0
        )
        for piece in range(PIECES)
    ]
    prompt_count = prompt_length.shape[0] // group_count
    seg_rows = tok_rows // prompt_count
    first_prompt = group * prompt_count
    my_lengths = lax.dynamic_slice_in_dim(prompt_length, first_prompt, prompt_count)
    my_prefix = lax.dynamic_slice_in_dim(prefix_read_length, first_prompt, prompt_count)
    token_prefix = jnp.repeat(my_prefix, seg_rows, total_repeat_length=tok_rows)
    context = local_attention(
        queries, prefix_key_cache, prefix_value_cache, prompt_keys, prompt_values, token_prefix
    )
    token_length = jnp.repeat(my_lengths, seg_rows, total_repeat_length=tok_rows)
    live_rows = jnp.arange(tok_rows, dtype=jnp.int32) % seg_rows < token_length
    context = context * live_rows.astype(jnp.bfloat16)[:, None]
    adapter_count = adapter_row_map.shape[0]
    adapter_local_row = adapter_down_weight.shape[0]
    matches = prompt_adapter[:, None] == jnp.arange(adapter_count, dtype=jnp.int32)[None, :]
    stored_all = jnp.sum(jnp.where(matches, adapter_row_map[None, :], 0), axis=1)
    owners = (stored_all // adapter_local_row).reshape(group_count, prompt_count)
    local_rows = (stored_all % adapter_local_row).reshape(group_count, prompt_count)
    same_owner = owners[:, :, None] == owners[:, None, :]
    earlier = jnp.arange(prompt_count)[None, None, :] < jnp.arange(prompt_count)[None, :, None]
    slots = jnp.sum(same_owner & earlier, axis=2)
    my_owner = lax.dynamic_index_in_dim(owners, group, 0, keepdims=False)
    my_slot = lax.dynamic_index_in_dim(slots, group, 0, keepdims=False)
    context_seg = context.reshape(prompt_count, seg_rows, query_width)
    owner_ids = jnp.arange(group_count, dtype=jnp.int32)
    slot_ids = jnp.arange(CAP, dtype=jnp.int32)
    give_mask = (owners == group)[:, None, :] & (slots[:, None, :] == slot_ids[None, :, None])
    which_give = jnp.sum(jnp.where(give_mask, local_rows[:, None, :], 0), axis=2)
    down_send, up_send = selected_blocks(which_give, adapter_down_weight, adapter_up_weight)
    down_recv, up_recv = (
        lax.all_to_all(down_send, "dp", split_axis=0, concat_axis=0, tiled=True),
        lax.all_to_all(up_send, "dp", split_axis=0, concat_axis=0, tiled=True),
    )
    take = (
        (my_owner[:, None, None] == owner_ids[None, :, None])
        & (my_slot[:, None, None] == slot_ids[None, None, :])
    ).astype(jnp.bfloat16)
    down_mine = jnp.einsum(
        "sdc,dcrf->srf", take, down_recv, preferred_element_type=jnp.float32
    ).astype(jnp.bfloat16)
    up_mine = jnp.einsum("sdc,dcro->sro", take, up_recv, preferred_element_type=jnp.float32).astype(
        jnp.bfloat16
    )
    lowrank = rank_total(
        jnp.einsum("sxf,srf->sxr", context_seg, down_mine, preferred_element_type=jnp.float32)
    ).astype(jnp.bfloat16)
    adapter_delta = jnp.einsum(
        "sxr,sro->sxo", lowrank, up_mine, preferred_element_type=jnp.float32
    ).astype(jnp.bfloat16)
    adapter_delta = adapter_delta.reshape(tok_rows, adapter_delta.shape[-1])
    context, adapter_delta = lax.optimization_barrier((context, adapter_delta))
    context_parts = context.reshape(tok_rows, part_count * half_rows)
    pieces = []
    for gathered in gathered_weights:
        blocks = gathered.reshape(group_count, query_width, piece_width)
        partial_value = jnp.concatenate(
            [
                jnp.dot(context_parts, blocks[index], preferred_element_type=jnp.float32)
                for index in range(group_count)
            ],
            axis=1,
        )
        summed = lax.psum_scatter(
            partial_value.astype(jnp.bfloat16), "tensor", scatter_dimension=1, tiled=True
        )
        pieces.append(summed.reshape(tok_rows, -1, 1, piece_width))
    base_output = jnp.concatenate(pieces, axis=2).reshape(tok_rows, -1).astype(jnp.float32)
    projected = base_output + adapter_scale * adapter_delta.astype(jnp.float32)
    return projected.astype(jnp.bfloat16)


def solution(mesh):
    in_specs = (
        P(("parts", "dp"), "tensor"),
        P("parts", "tensor"),
        P("parts", "tensor"),
        P(("parts", "dp"), "tensor"),
        P(("parts", "dp"), "tensor"),
        P("tensor", "dp"),
        P(("parts", "dp"), None, "tensor"),
        P(("parts", "dp"), None, "tensor"),
        P("parts"),
        P("parts"),
        P("parts"),
        P("parts"),
    )
    out_specs = P(("parts", "dp"), "tensor")
    return jax.shard_map(local, mesh=mesh, in_specs=in_specs, out_specs=out_specs, check_vma=False)
```

```python
import jax
import jax.numpy as jnp
from jax import lax
from jax.sharding import PartitionSpec as P

HD = 128
CAP = 1
PIECES = 2


adapter_scale = 2.0


def rank_total(partial_value):
    return lax.psum(partial_value, "tensor")


def local_attention(
    queries, prefix_key_cache, prefix_value_cache, prompt_keys, prompt_values, token_prefix
):
    tok_rows, query_width = queries.shape
    positions, key_width = prefix_key_cache.shape
    local_kv = key_width // HD
    group_size = query_width // key_width
    scale = HD ** (-0.5)
    query_four = queries.reshape(tok_rows, local_kv, group_size, HD)
    cache_keys = prefix_key_cache.reshape(positions, local_kv, HD)
    cache_values = prefix_value_cache.reshape(positions, local_kv, HD)
    own_key_heads = prompt_keys.reshape(tok_rows, local_kv, HD)
    own_value_heads = prompt_values.reshape(tok_rows, local_kv, HD)
    scores = (
        jnp.einsum("tkgd,pkd->kgtp", query_four, cache_keys, preferred_element_type=jnp.float32)
        * scale
    )
    own_score = (
        jnp.einsum("tkgd,tkd->kgt", query_four, own_key_heads, preferred_element_type=jnp.float32)
        * scale
    )
    valid = jnp.arange(positions, dtype=jnp.int32)[None, :] < token_prefix[:, None]
    scores = jnp.where(valid[None, None], scores, -jnp.inf)
    highest = jnp.maximum(jnp.max(scores, axis=-1), own_score)
    expon = jnp.exp(scores - highest[..., None])
    own_expon = jnp.exp(own_score - highest)
    total = jnp.sum(expon, axis=-1) + own_expon
    weights = (expon / total[..., None]).astype(jnp.bfloat16)
    own_weight = (own_expon / total).astype(jnp.bfloat16)
    context = jnp.einsum(
        "kgtp,pkd->tkgd", weights, cache_values, preferred_element_type=jnp.float32
    )
    context = context + jnp.einsum(
        "kgt,tkd->tkgd", own_weight, own_value_heads, preferred_element_type=jnp.float32
    )
    return context.reshape(tok_rows, query_width).astype(jnp.bfloat16)


def selected_blocks(local_adapter_index, adapter_down_weight, adapter_up_weight):
    adapter_number = adapter_down_weight.shape[0]
    adapter_selector = (
        local_adapter_index[..., None] == jnp.arange(adapter_number, dtype=jnp.int32)
    ).astype(jnp.bfloat16)
    down_selected = jnp.einsum(
        "ljm,mes->ljes", adapter_selector, adapter_down_weight, preferred_element_type=jnp.float32
    ).astype(jnp.bfloat16)
    up_selected = jnp.einsum(
        "yuv,vzj->yuzj", adapter_selector, adapter_up_weight, preferred_element_type=jnp.float32
    ).astype(jnp.bfloat16)
    return (down_selected, up_selected)


def chain_gather(pieces_in):
    group = lax.axis_index("dp")
    up = [(0, 1), (1, 2), (2, 3)]
    down = [(1, 0), (2, 1), (3, 2)]
    swap = [(0, 1), (1, 0)]
    count = len(pieces_in)
    from_low = list(pieces_in)
    from_high = list(pieces_in)
    first_high = [None] * count
    slots = [[] for _ in range(count)]
    for step in range(1, 4):
        for piece in range(count):
            from_low[piece] = lax.ppermute(from_low[piece], "dp", up)
            from_high[piece] = lax.ppermute(from_high[piece], "dp", down)
            low, high = from_low[piece], from_high[piece]
            if step == 1:
                first_high[piece] = high
                mine = jnp.where(group >= 1, low, high)
            elif step == 2:
                mine = jnp.where(group >= 2, low, high)
            else:
                mine = jnp.where(
                    group == 3, low, jnp.where(group == 0, high, first_high[piece])
                )
            slots[piece].append((mine, lax.ppermute(mine, "parts", swap)))
    return slots


def chain_project(context, own, slots):
    group = lax.axis_index("dp")
    part = lax.axis_index("parts")
    tensor = lax.axis_index("tensor")
    core, chip = tensor % 2, tensor // 2
    half = own.shape[0] // 2
    context_mine = lax.dynamic_slice_in_dim(context, part * half, half, axis=1)
    context_other = lax.dynamic_slice_in_dim(context, (1 - part) * half, half, axis=1)
    results = [jnp.dot(context, own, preferred_element_type=jnp.float32).astype(jnp.bfloat16)]
    for mine, other in slots:
        value = jnp.dot(context_mine, mine, preferred_element_type=jnp.float32)
        value = value + jnp.dot(context_other, other, preferred_element_type=jnp.float32)
        results.append(value.astype(jnp.bfloat16))
    stack = jnp.stack(results)
    first = jnp.where(group >= 1, group - 1, 1)
    second = jnp.where(group >= 2, group - 2, group + 2)
    third = jnp.where(group == 3, 0, jnp.where(group == 0, 3, group + 1))
    order = jnp.stack([group, first, second, third])

    def block(index):
        slot = jnp.sum(jnp.where(order == index, jnp.arange(4, dtype=jnp.int32), 0))
        return lax.dynamic_index_in_dim(stack, slot, 0, keepdims=False)

    core_swap = [(0, 1), (1, 0), (2, 3), (3, 2)]
    chip_swap = [(0, 2), (2, 0), (1, 3), (3, 1)]
    far = jnp.stack([block(1 - core), block(3 - core)])
    far = lax.ppermute(far, "tensor", core_swap).astype(jnp.float32)
    near = jnp.stack([block(core), block(2 + core)]).astype(jnp.float32) + far
    sent = lax.dynamic_index_in_dim(near, 1 - chip, 0, keepdims=False).astype(jnp.bfloat16)
    kept = lax.dynamic_index_in_dim(near, chip, 0, keepdims=False)
    return kept + lax.ppermute(sent, "tensor", chip_swap).astype(jnp.float32)


def local(
    queries,
    prefix_key_cache,
    prefix_value_cache,
    prompt_keys,
    prompt_values,
    output_weight,
    adapter_down_weight,
    adapter_up_weight,
    adapter_row_map,
    prompt_adapter,
    prompt_length,
    prefix_read_length,
):
    group_count = lax.axis_size("dp")
    group = lax.axis_index("dp")
    tok_rows, query_width = queries.shape
    part_count = lax.axis_size("parts")
    half_rows = query_width // part_count
    piece_width = output_weight.shape[1] // PIECES
    half_weight = lax.dynamic_slice_in_dim(
        output_weight, lax.axis_index("parts") * half_rows, half_rows, axis=0
    )
    pieces_in = [
        half_weight[:, piece * piece_width : (piece + 1) * piece_width] for piece in range(PIECES)
    ]
    chained = group_count == 4 and part_count == 2 and lax.axis_size("tensor") == 4
    if chained:
        gathered_weights = chain_gather(pieces_in)
    else:
        gathered_weights = [lax.all_gather(piece, ("dp", "parts"), axis=0) for piece in pieces_in]
    prompt_count = prompt_length.shape[0] // group_count
    seg_rows = tok_rows // prompt_count
    first_prompt = group * prompt_count
    my_lengths = lax.dynamic_slice_in_dim(prompt_length, first_prompt, prompt_count)
    my_prefix = lax.dynamic_slice_in_dim(prefix_read_length, first_prompt, prompt_count)
    token_prefix = jnp.repeat(my_prefix, seg_rows, total_repeat_length=tok_rows)
    context = local_attention(
        queries, prefix_key_cache, prefix_value_cache, prompt_keys, prompt_values, token_prefix
    )
    token_length = jnp.repeat(my_lengths, seg_rows, total_repeat_length=tok_rows)
    live_rows = jnp.arange(tok_rows, dtype=jnp.int32) % seg_rows < token_length
    context = context * live_rows.astype(jnp.bfloat16)[:, None]
    adapter_count = adapter_row_map.shape[0]
    adapter_local_row = adapter_down_weight.shape[0]
    matches = prompt_adapter[:, None] == jnp.arange(adapter_count, dtype=jnp.int32)[None, :]
    stored_all = jnp.sum(jnp.where(matches, adapter_row_map[None, :], 0), axis=1)
    owners = (stored_all // adapter_local_row).reshape(group_count, prompt_count)
    local_rows = (stored_all % adapter_local_row).reshape(group_count, prompt_count)
    same_owner = owners[:, :, None] == owners[:, None, :]
    earlier = jnp.arange(prompt_count)[None, None, :] < jnp.arange(prompt_count)[None, :, None]
    slots = jnp.sum(same_owner & earlier, axis=2)
    my_owner = lax.dynamic_index_in_dim(owners, group, 0, keepdims=False)
    my_slot = lax.dynamic_index_in_dim(slots, group, 0, keepdims=False)
    context_seg = context.reshape(prompt_count, seg_rows, query_width)
    owner_ids = jnp.arange(group_count, dtype=jnp.int32)
    slot_ids = jnp.arange(CAP, dtype=jnp.int32)
    give_mask = (owners == group)[:, None, :] & (slots[:, None, :] == slot_ids[None, :, None])
    which_give = jnp.sum(jnp.where(give_mask, local_rows[:, None, :], 0), axis=2)
    down_send, up_send = selected_blocks(which_give, adapter_down_weight, adapter_up_weight)
    down_recv, up_recv = (
        lax.all_to_all(down_send, "dp", split_axis=0, concat_axis=0, tiled=True),
        lax.all_to_all(up_send, "dp", split_axis=0, concat_axis=0, tiled=True),
    )
    take = (
        (my_owner[:, None, None] == owner_ids[None, :, None])
        & (my_slot[:, None, None] == slot_ids[None, None, :])
    ).astype(jnp.bfloat16)
    down_mine = jnp.einsum(
        "sdc,dcrf->srf", take, down_recv, preferred_element_type=jnp.float32
    ).astype(jnp.bfloat16)
    up_mine = jnp.einsum("sdc,dcro->sro", take, up_recv, preferred_element_type=jnp.float32).astype(
        jnp.bfloat16
    )
    lowrank = rank_total(
        jnp.einsum("sxf,srf->sxr", context_seg, down_mine, preferred_element_type=jnp.float32)
    ).astype(jnp.bfloat16)
    adapter_delta = jnp.einsum(
        "sxr,sro->sxo", lowrank, up_mine, preferred_element_type=jnp.float32
    ).astype(jnp.bfloat16)
    adapter_delta = adapter_delta.reshape(tok_rows, adapter_delta.shape[-1])
    context, adapter_delta = lax.optimization_barrier((context, adapter_delta))
    pieces = []
    for piece, gathered in enumerate(gathered_weights):
        if chained:
            own = output_weight[:, piece * piece_width : (piece + 1) * piece_width]
            summed = chain_project(context, own, gathered)
        else:
            blocks = gathered.reshape(group_count, query_width, piece_width)
            partial_value = jnp.einsum(
                "tf,dfc->tdc", context, blocks, preferred_element_type=jnp.float32
            ).reshape(tok_rows, -1)
            summed = lax.psum_scatter(partial_value, "tensor", scatter_dimension=1, tiled=True)
        pieces.append(summed.reshape(tok_rows, -1, 1, piece_width))
    base_output = jnp.concatenate(pieces, axis=2).reshape(tok_rows, -1)
    projected = base_output + adapter_scale * adapter_delta.astype(jnp.float32)
    return projected.astype(jnp.bfloat16)


def solution(mesh):
    in_specs = (
        P(("parts", "dp"), "tensor"),
        P("parts", "tensor"),
        P("parts", "tensor"),
        P(("parts", "dp"), "tensor"),
        P(("parts", "dp"), "tensor"),
        P("tensor", "dp"),
        P(("parts", "dp"), None, "tensor"),
        P(("parts", "dp"), None, "tensor"),
        P("parts"),
        P("parts"),
        P("parts"),
        P("parts"),
    )
    out_specs = P(("parts", "dp"), "tensor")
    return jax.shard_map(local, mesh=mesh, in_specs=in_specs, out_specs=out_specs, check_vma=False)
```

```python
import jax
import jax.numpy as jnp
from jax import lax
from jax.sharding import PartitionSpec as P

HD = 128
CAP = 1
PIECES = 2


adapter_scale = 2.0


def rank_total(partial_value):
    return lax.psum(partial_value, "tensor")


def local_attention(
    queries, prefix_key_cache, prefix_value_cache, prompt_keys, prompt_values, token_prefix
):
    tok_rows, query_width = queries.shape
    positions, key_width = prefix_key_cache.shape
    local_kv = key_width // HD
    group_size = query_width // key_width
    scale = HD ** (-0.5)
    query_four = queries.reshape(tok_rows, local_kv, group_size, HD)
    cache_keys = prefix_key_cache.reshape(positions, local_kv, HD)
    cache_values = prefix_value_cache.reshape(positions, local_kv, HD)
    own_key_heads = prompt_keys.reshape(tok_rows, local_kv, HD)
    own_value_heads = prompt_values.reshape(tok_rows, local_kv, HD)
    scores = (
        jnp.einsum("tkgd,pkd->kgtp", query_four, cache_keys, preferred_element_type=jnp.float32)
        * scale
    )
    own_score = (
        jnp.einsum("tkgd,tkd->kgt", query_four, own_key_heads, preferred_element_type=jnp.float32)
        * scale
    )
    valid = jnp.arange(positions, dtype=jnp.int32)[None, :] < token_prefix[:, None]
    scores = jnp.where(valid[None, None], scores, -jnp.inf)
    highest = jnp.maximum(jnp.max(scores, axis=-1), own_score)
    expon = jnp.exp(scores - highest[..., None])
    own_expon = jnp.exp(own_score - highest)
    total = jnp.sum(expon, axis=-1) + own_expon
    weights = (expon / total[..., None]).astype(jnp.bfloat16)
    own_weight = (own_expon / total).astype(jnp.bfloat16)
    context = jnp.einsum(
        "kgtp,pkd->tkgd", weights, cache_values, preferred_element_type=jnp.float32
    )
    context = context + jnp.einsum(
        "kgt,tkd->tkgd", own_weight, own_value_heads, preferred_element_type=jnp.float32
    )
    return context.reshape(tok_rows, query_width).astype(jnp.bfloat16)


def selected_blocks(local_adapter_index, adapter_down_weight, adapter_up_weight):
    adapter_number = adapter_down_weight.shape[0]
    adapter_selector = (
        local_adapter_index[..., None] == jnp.arange(adapter_number, dtype=jnp.int32)
    ).astype(jnp.bfloat16)
    down_selected = jnp.einsum(
        "ljm,mes->ljes", adapter_selector, adapter_down_weight, preferred_element_type=jnp.float32
    ).astype(jnp.bfloat16)
    up_selected = jnp.einsum(
        "yuv,vzj->yuzj", adapter_selector, adapter_up_weight, preferred_element_type=jnp.float32
    ).astype(jnp.bfloat16)
    return (down_selected, up_selected)


def chain_gather(pieces_in, units):
    group = lax.axis_index("dp")
    up = [(0, 1), (1, 2), (2, 3)]
    down = [(1, 0), (2, 1), (3, 2)]
    swap = [(0, 1), (1, 0)]
    count = len(pieces_in)
    units = list(units)
    from_low = [lax.ppermute(piece, "dp", up) for piece in pieces_in]
    from_high = [lax.ppermute(piece, "dp", down) for piece in pieces_in]
    first_high = list(from_high)
    slots = [[] for _ in range(count)]
    next_unit = 2
    for step in range(1, 4):
        for piece in range(count):
            low, high = lax.optimization_barrier((from_low[piece], from_high[piece]))
            if step == 1:
                first_high[piece] = high
                mine = jnp.where(group >= 1, low, high)
            elif step == 2:
                mine = jnp.where(group >= 2, low, high)
            else:
                mine = jnp.where(
                    group == 3, low, jnp.where(group == 0, high, first_high[piece])
                )
            if step > 1:
                before, other = slots[piece][-1]
                mine, low, high, other = lax.optimization_barrier((mine, low, high, other))
                slots[piece][-1] = (before, other)
            else:
                mine, low, high = lax.optimization_barrier((mine, low, high))
            if next_unit < len(units) and step > 1 and piece == 0:
                units[next_unit], mine, low, high = lax.optimization_barrier(
                    (units[next_unit], mine, low, high)
                )
                next_unit += 1
            slots[piece].append((mine, lax.ppermute(mine, "parts", swap)))
            if step < 3:
                from_low[piece] = lax.ppermute(low, "dp", up)
                from_high[piece] = lax.ppermute(high, "dp", down)
    return slots, units


def chain_project(context, own, slots):
    group = lax.axis_index("dp")
    part = lax.axis_index("parts")
    tensor = lax.axis_index("tensor")
    core, chip = tensor % 2, tensor // 2
    half = own.shape[0] // 2
    context_mine = lax.dynamic_slice_in_dim(context, part * half, half, axis=1)
    context_other = lax.dynamic_slice_in_dim(context, (1 - part) * half, half, axis=1)
    results = [jnp.dot(context, own, preferred_element_type=jnp.float32).astype(jnp.bfloat16)]
    for mine, other in slots:
        value = jnp.dot(context_mine, mine, preferred_element_type=jnp.float32)
        value = value + jnp.dot(context_other, other, preferred_element_type=jnp.float32)
        results.append(value.astype(jnp.bfloat16))
    stack = jnp.stack(results)
    first = jnp.where(group >= 1, group - 1, 1)
    second = jnp.where(group >= 2, group - 2, group + 2)
    third = jnp.where(group == 3, 0, jnp.where(group == 0, 3, group + 1))
    order = jnp.stack([group, first, second, third])

    def block(index):
        slot = jnp.sum(jnp.where(order == index, jnp.arange(4, dtype=jnp.int32), 0))
        return lax.dynamic_index_in_dim(stack, slot, 0, keepdims=False)

    core_swap = [(0, 1), (1, 0), (2, 3), (3, 2)]
    chip_swap = [(0, 2), (2, 0), (1, 3), (3, 1)]
    far = jnp.stack([block(1 - core), block(3 - core)])
    far = lax.ppermute(far, "tensor", core_swap).astype(jnp.float32)
    near = jnp.stack([block(core), block(2 + core)]).astype(jnp.float32) + far
    sent = lax.dynamic_index_in_dim(near, 1 - chip, 0, keepdims=False).astype(jnp.bfloat16)
    kept = lax.dynamic_index_in_dim(near, chip, 0, keepdims=False)
    return kept + lax.ppermute(sent, "tensor", chip_swap).astype(jnp.float32)


def local(
    queries,
    prefix_key_cache,
    prefix_value_cache,
    prompt_keys,
    prompt_values,
    output_weight,
    adapter_down_weight,
    adapter_up_weight,
    adapter_row_map,
    prompt_adapter,
    prompt_length,
    prefix_read_length,
):
    group_count = lax.axis_size("dp")
    group = lax.axis_index("dp")
    tok_rows, query_width = queries.shape
    part_count = lax.axis_size("parts")
    half_rows = query_width // part_count
    piece_width = output_weight.shape[1] // PIECES
    half_weight = lax.dynamic_slice_in_dim(
        output_weight, lax.axis_index("parts") * half_rows, half_rows, axis=0
    )
    pieces_in = [
        half_weight[:, piece * piece_width : (piece + 1) * piece_width] for piece in range(PIECES)
    ]
    chained = group_count == 4 and part_count == 2 and lax.axis_size("tensor") == 4
    prompt_count = prompt_length.shape[0] // group_count
    seg_rows = tok_rows // prompt_count
    first_prompt = group * prompt_count
    my_lengths = lax.dynamic_slice_in_dim(prompt_length, first_prompt, prompt_count)
    my_prefix = lax.dynamic_slice_in_dim(prefix_read_length, first_prompt, prompt_count)
    token_prefix = jnp.repeat(my_prefix, seg_rows, total_repeat_length=tok_rows)
    if chained:
        local_kv = prefix_key_cache.shape[1] // HD
        heads_width = query_width // local_kv
        units = []
        for prompt in range(prompt_count):
            rows = slice(prompt * seg_rows, (prompt + 1) * seg_rows)
            for head in range(local_kv):
                columns = slice(head * HD, (head + 1) * HD)
                units.append(
                    (
                        queries[rows, head * heads_width : (head + 1) * heads_width],
                        prefix_key_cache[:, columns],
                        prefix_value_cache[:, columns],
                        prompt_keys[rows, columns],
                        prompt_values[rows, columns],
                        token_prefix[rows],
                    )
                )
        gathered_weights, units = chain_gather(pieces_in, units)
        outs = [local_attention(*unit) for unit in units]
        context = jnp.concatenate(
            [
                jnp.concatenate(outs[prompt * local_kv : (prompt + 1) * local_kv], axis=1)
                for prompt in range(prompt_count)
            ],
            axis=0,
        )
    else:
        gathered_weights = [lax.all_gather(piece, ("dp", "parts"), axis=0) for piece in pieces_in]
        context = local_attention(
            queries, prefix_key_cache, prefix_value_cache, prompt_keys, prompt_values, token_prefix
        )
    token_length = jnp.repeat(my_lengths, seg_rows, total_repeat_length=tok_rows)
    live_rows = jnp.arange(tok_rows, dtype=jnp.int32) % seg_rows < token_length
    context = context * live_rows.astype(jnp.bfloat16)[:, None]
    adapter_count = adapter_row_map.shape[0]
    adapter_local_row = adapter_down_weight.shape[0]
    matches = prompt_adapter[:, None] == jnp.arange(adapter_count, dtype=jnp.int32)[None, :]
    stored_all = jnp.sum(jnp.where(matches, adapter_row_map[None, :], 0), axis=1)
    owners = (stored_all // adapter_local_row).reshape(group_count, prompt_count)
    local_rows = (stored_all % adapter_local_row).reshape(group_count, prompt_count)
    same_owner = owners[:, :, None] == owners[:, None, :]
    earlier = jnp.arange(prompt_count)[None, None, :] < jnp.arange(prompt_count)[None, :, None]
    slots = jnp.sum(same_owner & earlier, axis=2)
    my_owner = lax.dynamic_index_in_dim(owners, group, 0, keepdims=False)
    my_slot = lax.dynamic_index_in_dim(slots, group, 0, keepdims=False)
    context_seg = context.reshape(prompt_count, seg_rows, query_width)
    owner_ids = jnp.arange(group_count, dtype=jnp.int32)
    slot_ids = jnp.arange(CAP, dtype=jnp.int32)
    give_mask = (owners == group)[:, None, :] & (slots[:, None, :] == slot_ids[None, :, None])
    which_give = jnp.sum(jnp.where(give_mask, local_rows[:, None, :], 0), axis=2)
    down_send, up_send = selected_blocks(which_give, adapter_down_weight, adapter_up_weight)
    down_recv, up_recv = (
        lax.all_to_all(down_send, "dp", split_axis=0, concat_axis=0, tiled=True),
        lax.all_to_all(up_send, "dp", split_axis=0, concat_axis=0, tiled=True),
    )
    take = (
        (my_owner[:, None, None] == owner_ids[None, :, None])
        & (my_slot[:, None, None] == slot_ids[None, None, :])
    ).astype(jnp.bfloat16)
    down_mine = jnp.einsum(
        "sdc,dcrf->srf", take, down_recv, preferred_element_type=jnp.float32
    ).astype(jnp.bfloat16)
    up_mine = jnp.einsum("sdc,dcro->sro", take, up_recv, preferred_element_type=jnp.float32).astype(
        jnp.bfloat16
    )
    lowrank = rank_total(
        jnp.einsum("sxf,srf->sxr", context_seg, down_mine, preferred_element_type=jnp.float32)
    ).astype(jnp.bfloat16)
    adapter_delta = jnp.einsum(
        "sxr,sro->sxo", lowrank, up_mine, preferred_element_type=jnp.float32
    ).astype(jnp.bfloat16)
    adapter_delta = adapter_delta.reshape(tok_rows, adapter_delta.shape[-1])
    context, adapter_delta = lax.optimization_barrier((context, adapter_delta))
    pieces = []
    for piece, gathered in enumerate(gathered_weights):
        if chained:
            own = output_weight[:, piece * piece_width : (piece + 1) * piece_width]
            summed = chain_project(context, own, gathered)
        else:
            blocks = gathered.reshape(group_count, query_width, piece_width)
            partial_value = jnp.einsum(
                "tf,dfc->tdc", context, blocks, preferred_element_type=jnp.float32
            ).reshape(tok_rows, -1)
            summed = lax.psum_scatter(partial_value, "tensor", scatter_dimension=1, tiled=True)
        pieces.append(summed.reshape(tok_rows, -1, 1, piece_width))
    base_output = jnp.concatenate(pieces, axis=2).reshape(tok_rows, -1)
    projected = base_output + adapter_scale * adapter_delta.astype(jnp.float32)
    return projected.astype(jnp.bfloat16)


def solution(mesh):
    in_specs = (
        P(("parts", "dp"), "tensor"),
        P("parts", "tensor"),
        P("parts", "tensor"),
        P(("parts", "dp"), "tensor"),
        P(("parts", "dp"), "tensor"),
        P("tensor", "dp"),
        P(("parts", "dp"), None, "tensor"),
        P(("parts", "dp"), None, "tensor"),
        P("parts"),
        P("parts"),
        P("parts"),
        P("parts"),
    )
    out_specs = P(("parts", "dp"), "tensor")
    return jax.shard_map(local, mesh=mesh, in_specs=in_specs, out_specs=out_specs, check_vma=False)
```

```python
import jax
import jax.numpy as jnp
from jax import lax
from jax.sharding import PartitionSpec as P

HD = 128
CAP = 1
PIECES = 2


adapter_scale = 2.0


def rank_total(partial_value):
    return lax.psum(partial_value, "tensor")


def local_attention(
    queries, prefix_key_cache, prefix_value_cache, prompt_keys, prompt_values, token_prefix
):
    tok_rows, query_width = queries.shape
    positions, key_width = prefix_key_cache.shape
    local_kv = key_width // HD
    group_size = query_width // key_width
    scale = HD ** (-0.5)
    query_four = queries.reshape(tok_rows, local_kv, group_size, HD)
    cache_keys = prefix_key_cache.reshape(positions, local_kv, HD)
    cache_values = prefix_value_cache.reshape(positions, local_kv, HD)
    own_key_heads = prompt_keys.reshape(tok_rows, local_kv, HD)
    own_value_heads = prompt_values.reshape(tok_rows, local_kv, HD)
    scores = (
        jnp.einsum("tkgd,pkd->kgtp", query_four, cache_keys, preferred_element_type=jnp.float32)
        * scale
    )
    own_score = (
        jnp.einsum("tkgd,tkd->kgt", query_four, own_key_heads, preferred_element_type=jnp.float32)
        * scale
    )
    valid = jnp.arange(positions, dtype=jnp.int32)[None, :] < token_prefix[:, None]
    scores = jnp.where(valid[None, None], scores, -jnp.inf)
    highest = jnp.maximum(jnp.max(scores, axis=-1), own_score)
    expon = jnp.exp(scores - highest[..., None])
    own_expon = jnp.exp(own_score - highest)
    total = jnp.sum(expon, axis=-1) + own_expon
    weights = (expon / total[..., None]).astype(jnp.bfloat16)
    own_weight = (own_expon / total).astype(jnp.bfloat16)
    context = jnp.einsum(
        "kgtp,pkd->tkgd", weights, cache_values, preferred_element_type=jnp.float32
    )
    context = context + jnp.einsum(
        "kgt,tkd->tkgd", own_weight, own_value_heads, preferred_element_type=jnp.float32
    )
    return context.reshape(tok_rows, query_width).astype(jnp.bfloat16)


def selected_blocks(local_adapter_index, adapter_down_weight, adapter_up_weight):
    adapter_number = adapter_down_weight.shape[0]
    adapter_selector = (
        local_adapter_index[..., None] == jnp.arange(adapter_number, dtype=jnp.int32)
    ).astype(jnp.bfloat16)
    down_selected = jnp.einsum(
        "ljm,mes->ljes", adapter_selector, adapter_down_weight, preferred_element_type=jnp.float32
    ).astype(jnp.bfloat16)
    up_selected = jnp.einsum(
        "yuv,vzj->yuzj", adapter_selector, adapter_up_weight, preferred_element_type=jnp.float32
    ).astype(jnp.bfloat16)
    return (down_selected, up_selected)


def chain_gather(pieces_in, units):
    group = lax.axis_index("dp")
    up = [(0, 1), (1, 2), (2, 3)]
    down = [(1, 0), (2, 1), (3, 2)]
    swap = [(0, 1), (1, 0)]
    count = len(pieces_in)
    units = list(units)
    from_low = [lax.ppermute(piece, "dp", up) for piece in pieces_in]
    from_high = [lax.ppermute(piece, "dp", down) for piece in pieces_in]
    first_high = list(from_high)
    slots = [[] for _ in range(count)]
    next_unit = 1
    for step in range(1, 4):
        for piece in range(count):
            low, high = lax.optimization_barrier((from_low[piece], from_high[piece]))
            if step == 1:
                first_high[piece] = high
                mine = jnp.where(group >= 1, low, high)
            elif step == 2:
                mine = jnp.where(group >= 2, low, high)
            else:
                mine = jnp.where(
                    group == 3, low, jnp.where(group == 0, high, first_high[piece])
                )
            if step > 1:
                before, other = slots[piece][-1]
                mine, low, high, other = lax.optimization_barrier((mine, low, high, other))
                slots[piece][-1] = (before, other)
            else:
                mine, low, high = lax.optimization_barrier((mine, low, high))
            if next_unit < len(units) and step > 1:
                units[next_unit], mine, low, high = lax.optimization_barrier(
                    (units[next_unit], mine, low, high)
                )
                next_unit += 1
            slots[piece].append((mine, lax.ppermute(mine, "parts", swap)))
            if step < 3:
                from_low[piece] = lax.ppermute(low, "dp", up)
                from_high[piece] = lax.ppermute(high, "dp", down)
    return slots, units


def chain_project(context, own, slots):
    group = lax.axis_index("dp")
    part = lax.axis_index("parts")
    tensor = lax.axis_index("tensor")
    core, chip = tensor % 2, tensor // 2
    half = own.shape[0] // 2
    context_mine = lax.dynamic_slice_in_dim(context, part * half, half, axis=1)
    context_other = lax.dynamic_slice_in_dim(context, (1 - part) * half, half, axis=1)
    results = [jnp.dot(context, own, preferred_element_type=jnp.float32).astype(jnp.bfloat16)]
    for mine, other in slots:
        value = jnp.dot(context_mine, mine, preferred_element_type=jnp.float32)
        value = value + jnp.dot(context_other, other, preferred_element_type=jnp.float32)
        results.append(value.astype(jnp.bfloat16))
    stack = jnp.stack(results)
    first = jnp.where(group >= 1, group - 1, 1)
    second = jnp.where(group >= 2, group - 2, group + 2)
    third = jnp.where(group == 3, 0, jnp.where(group == 0, 3, group + 1))
    order = jnp.stack([group, first, second, third])

    def block(index):
        slot = jnp.sum(jnp.where(order == index, jnp.arange(4, dtype=jnp.int32), 0))
        return lax.dynamic_index_in_dim(stack, slot, 0, keepdims=False)

    core_swap = [(0, 1), (1, 0), (2, 3), (3, 2)]
    chip_swap = [(0, 2), (2, 0), (1, 3), (3, 1)]
    far = jnp.stack([block(1 - core), block(3 - core)])
    far = lax.ppermute(far, "tensor", core_swap).astype(jnp.float32)
    near = jnp.stack([block(core), block(2 + core)]).astype(jnp.float32) + far
    sent = lax.dynamic_index_in_dim(near, 1 - chip, 0, keepdims=False).astype(jnp.bfloat16)
    kept = lax.dynamic_index_in_dim(near, chip, 0, keepdims=False)
    return kept + lax.ppermute(sent, "tensor", chip_swap).astype(jnp.float32)


def local(
    queries,
    prefix_key_cache,
    prefix_value_cache,
    prompt_keys,
    prompt_values,
    output_weight,
    adapter_down_weight,
    adapter_up_weight,
    adapter_row_map,
    prompt_adapter,
    prompt_length,
    prefix_read_length,
):
    group_count = lax.axis_size("dp")
    group = lax.axis_index("dp")
    tok_rows, query_width = queries.shape
    part_count = lax.axis_size("parts")
    half_rows = query_width // part_count
    piece_width = output_weight.shape[1] // PIECES
    half_weight = lax.dynamic_slice_in_dim(
        output_weight, lax.axis_index("parts") * half_rows, half_rows, axis=0
    )
    pieces_in = [
        half_weight[:, piece * piece_width : (piece + 1) * piece_width] for piece in range(PIECES)
    ]
    chained = group_count == 4 and part_count == 2 and lax.axis_size("tensor") == 4
    prompt_count = prompt_length.shape[0] // group_count
    seg_rows = tok_rows // prompt_count
    first_prompt = group * prompt_count
    my_lengths = lax.dynamic_slice_in_dim(prompt_length, first_prompt, prompt_count)
    my_prefix = lax.dynamic_slice_in_dim(prefix_read_length, first_prompt, prompt_count)
    token_prefix = jnp.repeat(my_prefix, seg_rows, total_repeat_length=tok_rows)
    if chained:
        local_kv = prefix_key_cache.shape[1] // HD
        heads_width = query_width // local_kv
        units = []
        for prompt in range(prompt_count):
            rows = slice(prompt * seg_rows, (prompt + 1) * seg_rows)
            for head in range(local_kv):
                columns = slice(head * HD, (head + 1) * HD)
                units.append(
                    (
                        queries[rows, head * heads_width : (head + 1) * heads_width],
                        prefix_key_cache[:, columns],
                        prefix_value_cache[:, columns],
                        prompt_keys[rows, columns],
                        prompt_values[rows, columns],
                        token_prefix[rows],
                    )
                )
        gathered_weights, units = chain_gather(pieces_in, units)
        outs = [local_attention(*unit) for unit in units]
        context = jnp.concatenate(
            [
                jnp.concatenate(outs[prompt * local_kv : (prompt + 1) * local_kv], axis=1)
                for prompt in range(prompt_count)
            ],
            axis=0,
        )
    else:
        gathered_weights = [lax.all_gather(piece, ("dp", "parts"), axis=0) for piece in pieces_in]
        context = local_attention(
            queries, prefix_key_cache, prefix_value_cache, prompt_keys, prompt_values, token_prefix
        )
    token_length = jnp.repeat(my_lengths, seg_rows, total_repeat_length=tok_rows)
    live_rows = jnp.arange(tok_rows, dtype=jnp.int32) % seg_rows < token_length
    context = context * live_rows.astype(jnp.bfloat16)[:, None]
    if chained:
        mine, other = gathered_weights[0][-1]
        context, other = lax.optimization_barrier((context, other))
        gathered_weights[0][-1] = (mine, other)
    adapter_count = adapter_row_map.shape[0]
    adapter_local_row = adapter_down_weight.shape[0]
    matches = prompt_adapter[:, None] == jnp.arange(adapter_count, dtype=jnp.int32)[None, :]
    stored_all = jnp.sum(jnp.where(matches, adapter_row_map[None, :], 0), axis=1)
    owners = (stored_all // adapter_local_row).reshape(group_count, prompt_count)
    local_rows = (stored_all % adapter_local_row).reshape(group_count, prompt_count)
    same_owner = owners[:, :, None] == owners[:, None, :]
    earlier = jnp.arange(prompt_count)[None, None, :] < jnp.arange(prompt_count)[None, :, None]
    slots = jnp.sum(same_owner & earlier, axis=2)
    my_owner = lax.dynamic_index_in_dim(owners, group, 0, keepdims=False)
    my_slot = lax.dynamic_index_in_dim(slots, group, 0, keepdims=False)
    context_seg = context.reshape(prompt_count, seg_rows, query_width)
    owner_ids = jnp.arange(group_count, dtype=jnp.int32)
    slot_ids = jnp.arange(CAP, dtype=jnp.int32)
    give_mask = (owners == group)[:, None, :] & (slots[:, None, :] == slot_ids[None, :, None])
    which_give = jnp.sum(jnp.where(give_mask, local_rows[:, None, :], 0), axis=2)
    down_send, up_send = selected_blocks(which_give, adapter_down_weight, adapter_up_weight)
    down_recv, up_recv = (
        lax.all_to_all(down_send, "dp", split_axis=0, concat_axis=0, tiled=True),
        lax.all_to_all(up_send, "dp", split_axis=0, concat_axis=0, tiled=True),
    )
    take = (
        (my_owner[:, None, None] == owner_ids[None, :, None])
        & (my_slot[:, None, None] == slot_ids[None, None, :])
    ).astype(jnp.bfloat16)
    down_mine = jnp.einsum(
        "sdc,dcrf->srf", take, down_recv, preferred_element_type=jnp.float32
    ).astype(jnp.bfloat16)
    up_mine = jnp.einsum("sdc,dcro->sro", take, up_recv, preferred_element_type=jnp.float32).astype(
        jnp.bfloat16
    )
    lowrank = rank_total(
        jnp.einsum("sxf,srf->sxr", context_seg, down_mine, preferred_element_type=jnp.float32)
    ).astype(jnp.bfloat16)
    adapter_delta = jnp.einsum(
        "sxr,sro->sxo", lowrank, up_mine, preferred_element_type=jnp.float32
    ).astype(jnp.bfloat16)
    adapter_delta = adapter_delta.reshape(tok_rows, adapter_delta.shape[-1])
    context, adapter_delta = lax.optimization_barrier((context, adapter_delta))
    pieces = []
    for piece, gathered in enumerate(gathered_weights):
        if chained:
            own = output_weight[:, piece * piece_width : (piece + 1) * piece_width]
            summed = chain_project(context, own, gathered)
        else:
            blocks = gathered.reshape(group_count, query_width, piece_width)
            partial_value = jnp.einsum(
                "tf,dfc->tdc", context, blocks, preferred_element_type=jnp.float32
            ).reshape(tok_rows, -1)
            summed = lax.psum_scatter(partial_value, "tensor", scatter_dimension=1, tiled=True)
        pieces.append(summed.reshape(tok_rows, -1, 1, piece_width))
    base_output = jnp.concatenate(pieces, axis=2).reshape(tok_rows, -1)
    projected = base_output + adapter_scale * adapter_delta.astype(jnp.float32)
    return projected.astype(jnp.bfloat16)


def solution(mesh):
    in_specs = (
        P(("parts", "dp"), "tensor"),
        P("parts", "tensor"),
        P("parts", "tensor"),
        P(("parts", "dp"), "tensor"),
        P(("parts", "dp"), "tensor"),
        P("tensor", "dp"),
        P(("parts", "dp"), None, "tensor"),
        P(("parts", "dp"), None, "tensor"),
        P("parts"),
        P("parts"),
        P("parts"),
        P("parts"),
    )
    out_specs = P(("parts", "dp"), "tensor")
    return jax.shard_map(local, mesh=mesh, in_specs=in_specs, out_specs=out_specs, check_vma=False)
```

```python
import jax
import jax.numpy as jnp
from jax import lax
from jax.sharding import PartitionSpec as P

HD = 128
CAP = 1
PIECES = 2


adapter_scale = 2.0


def rank_total(partial_value):
    return lax.psum(partial_value, "tensor")


def local_attention(
    queries, prefix_key_cache, prefix_value_cache, prompt_keys, prompt_values, token_prefix
):
    tok_rows, query_width = queries.shape
    positions, key_width = prefix_key_cache.shape
    local_kv = key_width // HD
    group_size = query_width // key_width
    scale = HD ** (-0.5)
    query_four = queries.reshape(tok_rows, local_kv, group_size, HD)
    cache_keys = prefix_key_cache.reshape(positions, local_kv, HD)
    cache_values = prefix_value_cache.reshape(positions, local_kv, HD)
    own_key_heads = prompt_keys.reshape(tok_rows, local_kv, HD)
    own_value_heads = prompt_values.reshape(tok_rows, local_kv, HD)
    scores = (
        jnp.einsum("tkgd,pkd->kgtp", query_four, cache_keys, preferred_element_type=jnp.float32)
        * scale
    )
    own_score = (
        jnp.einsum("tkgd,tkd->kgt", query_four, own_key_heads, preferred_element_type=jnp.float32)
        * scale
    )
    valid = jnp.arange(positions, dtype=jnp.int32)[None, :] < token_prefix[:, None]
    scores = jnp.where(valid[None, None], scores, -jnp.inf)
    highest = jnp.maximum(jnp.max(scores, axis=-1), own_score)
    expon = jnp.exp(scores - highest[..., None])
    own_expon = jnp.exp(own_score - highest)
    total = jnp.sum(expon, axis=-1) + own_expon
    weights = (expon / total[..., None]).astype(jnp.bfloat16)
    own_weight = (own_expon / total).astype(jnp.bfloat16)
    context = jnp.einsum(
        "kgtp,pkd->tkgd", weights, cache_values, preferred_element_type=jnp.float32
    )
    context = context + jnp.einsum(
        "kgt,tkd->tkgd", own_weight, own_value_heads, preferred_element_type=jnp.float32
    )
    return context.reshape(tok_rows, query_width).astype(jnp.bfloat16)


def selected_blocks(local_adapter_index, adapter_down_weight, adapter_up_weight):
    adapter_number = adapter_down_weight.shape[0]
    adapter_selector = (
        local_adapter_index[..., None] == jnp.arange(adapter_number, dtype=jnp.int32)
    ).astype(jnp.bfloat16)
    down_selected = jnp.einsum(
        "ljm,mes->ljes", adapter_selector, adapter_down_weight, preferred_element_type=jnp.float32
    ).astype(jnp.bfloat16)
    up_selected = jnp.einsum(
        "yuv,vzj->yuzj", adapter_selector, adapter_up_weight, preferred_element_type=jnp.float32
    ).astype(jnp.bfloat16)
    return (down_selected, up_selected)


def chain_gather(pieces_in, units):
    group = lax.axis_index("dp")
    up = [(0, 1), (1, 2), (2, 3)]
    down = [(1, 0), (2, 1), (3, 2)]
    swap = [(0, 1), (1, 0)]
    count = len(pieces_in)
    units = list(units)
    from_low = [lax.ppermute(piece, "dp", up) for piece in pieces_in]
    from_high = [lax.ppermute(piece, "dp", down) for piece in pieces_in]
    first_high = list(from_high)
    slots = [[] for _ in range(count)]
    next_unit = 1
    for step in range(1, 4):
        for piece in range(count):
            low, high = lax.optimization_barrier((from_low[piece], from_high[piece]))
            if step == 1:
                first_high[piece] = high
                mine = jnp.where(group >= 1, low, high)
            elif step == 2:
                mine = jnp.where(group >= 2, low, high)
            else:
                mine = jnp.where(
                    group == 3, low, jnp.where(group == 0, high, first_high[piece])
                )
            if step > 1:
                before, other = slots[piece][-1]
                mine, low, high, other = lax.optimization_barrier((mine, low, high, other))
                slots[piece][-1] = (before, other)
            else:
                mine, low, high = lax.optimization_barrier((mine, low, high))
            last = len(units) if (step, piece) == (2, count - 1) else next_unit + 1
            while step > 1 and next_unit < min(last, len(units)):
                units[next_unit], mine, low, high = lax.optimization_barrier(
                    (units[next_unit], mine, low, high)
                )
                next_unit += 1
            slots[piece].append((mine, lax.ppermute(mine, "parts", swap)))
            if step < 3:
                from_low[piece] = lax.ppermute(low, "dp", up)
                from_high[piece] = lax.ppermute(high, "dp", down)
    return slots, units


def chain_project(context, own, slots):
    group = lax.axis_index("dp")
    part = lax.axis_index("parts")
    tensor = lax.axis_index("tensor")
    core, chip = tensor % 2, tensor // 2
    half = own.shape[0] // 2
    context_mine = lax.dynamic_slice_in_dim(context, part * half, half, axis=1)
    context_other = lax.dynamic_slice_in_dim(context, (1 - part) * half, half, axis=1)
    results = [jnp.dot(context, own, preferred_element_type=jnp.float32).astype(jnp.bfloat16)]
    for mine, other in slots:
        value = jnp.dot(context_mine, mine, preferred_element_type=jnp.float32)
        value = value + jnp.dot(context_other, other, preferred_element_type=jnp.float32)
        results.append(value.astype(jnp.bfloat16))
    stack = jnp.stack(results)
    first = jnp.where(group >= 1, group - 1, 1)
    second = jnp.where(group >= 2, group - 2, group + 2)
    third = jnp.where(group == 3, 0, jnp.where(group == 0, 3, group + 1))
    order = jnp.stack([group, first, second, third])

    def block(index):
        slot = jnp.sum(jnp.where(order == index, jnp.arange(4, dtype=jnp.int32), 0))
        return lax.dynamic_index_in_dim(stack, slot, 0, keepdims=False)

    core_swap = [(0, 1), (1, 0), (2, 3), (3, 2)]
    chip_swap = [(0, 2), (2, 0), (1, 3), (3, 1)]
    far = jnp.stack([block(1 - core), block(3 - core)])
    far = lax.ppermute(far, "tensor", core_swap).astype(jnp.float32)
    near = jnp.stack([block(core), block(2 + core)]).astype(jnp.float32) + far
    sent = lax.dynamic_index_in_dim(near, 1 - chip, 0, keepdims=False).astype(jnp.bfloat16)
    kept = lax.dynamic_index_in_dim(near, chip, 0, keepdims=False)
    return kept + lax.ppermute(sent, "tensor", chip_swap).astype(jnp.float32)


def local(
    queries,
    prefix_key_cache,
    prefix_value_cache,
    prompt_keys,
    prompt_values,
    output_weight,
    adapter_down_weight,
    adapter_up_weight,
    adapter_row_map,
    prompt_adapter,
    prompt_length,
    prefix_read_length,
):
    group_count = lax.axis_size("dp")
    group = lax.axis_index("dp")
    tok_rows, query_width = queries.shape
    part_count = lax.axis_size("parts")
    half_rows = query_width // part_count
    piece_width = output_weight.shape[1] // PIECES
    half_weight = lax.dynamic_slice_in_dim(
        output_weight, lax.axis_index("parts") * half_rows, half_rows, axis=0
    )
    pieces_in = [
        half_weight[:, piece * piece_width : (piece + 1) * piece_width] for piece in range(PIECES)
    ]
    chained = group_count == 4 and part_count == 2 and lax.axis_size("tensor") == 4
    prompt_count = prompt_length.shape[0] // group_count
    seg_rows = tok_rows // prompt_count
    first_prompt = group * prompt_count
    my_lengths = lax.dynamic_slice_in_dim(prompt_length, first_prompt, prompt_count)
    my_prefix = lax.dynamic_slice_in_dim(prefix_read_length, first_prompt, prompt_count)
    token_prefix = jnp.repeat(my_prefix, seg_rows, total_repeat_length=tok_rows)
    if chained:
        local_kv = prefix_key_cache.shape[1] // HD
        heads_width = query_width // local_kv
        units = []
        for prompt in range(prompt_count):
            rows = slice(prompt * seg_rows, (prompt + 1) * seg_rows)
            for head in range(local_kv):
                columns = slice(head * HD, (head + 1) * HD)
                units.append(
                    (
                        queries[rows, head * heads_width : (head + 1) * heads_width],
                        prefix_key_cache[:, columns],
                        prefix_value_cache[:, columns],
                        prompt_keys[rows, columns],
                        prompt_values[rows, columns],
                        token_prefix[rows],
                    )
                )
        gathered_weights, units = chain_gather(pieces_in, units)
        outs = [local_attention(*unit) for unit in units]
        context = jnp.concatenate(
            [
                jnp.concatenate(outs[prompt * local_kv : (prompt + 1) * local_kv], axis=1)
                for prompt in range(prompt_count)
            ],
            axis=0,
        )
    else:
        gathered_weights = [lax.all_gather(piece, ("dp", "parts"), axis=0) for piece in pieces_in]
        context = local_attention(
            queries, prefix_key_cache, prefix_value_cache, prompt_keys, prompt_values, token_prefix
        )
    token_length = jnp.repeat(my_lengths, seg_rows, total_repeat_length=tok_rows)
    live_rows = jnp.arange(tok_rows, dtype=jnp.int32) % seg_rows < token_length
    context = context * live_rows.astype(jnp.bfloat16)[:, None]
    adapter_count = adapter_row_map.shape[0]
    adapter_local_row = adapter_down_weight.shape[0]
    matches = prompt_adapter[:, None] == jnp.arange(adapter_count, dtype=jnp.int32)[None, :]
    stored_all = jnp.sum(jnp.where(matches, adapter_row_map[None, :], 0), axis=1)
    owners = (stored_all // adapter_local_row).reshape(group_count, prompt_count)
    local_rows = (stored_all % adapter_local_row).reshape(group_count, prompt_count)
    same_owner = owners[:, :, None] == owners[:, None, :]
    earlier = jnp.arange(prompt_count)[None, None, :] < jnp.arange(prompt_count)[None, :, None]
    slots = jnp.sum(same_owner & earlier, axis=2)
    my_owner = lax.dynamic_index_in_dim(owners, group, 0, keepdims=False)
    my_slot = lax.dynamic_index_in_dim(slots, group, 0, keepdims=False)
    context_seg = context.reshape(prompt_count, seg_rows, query_width)
    owner_ids = jnp.arange(group_count, dtype=jnp.int32)
    slot_ids = jnp.arange(CAP, dtype=jnp.int32)
    give_mask = (owners == group)[:, None, :] & (slots[:, None, :] == slot_ids[None, :, None])
    which_give = jnp.sum(jnp.where(give_mask, local_rows[:, None, :], 0), axis=2)
    down_send, up_send = selected_blocks(which_give, adapter_down_weight, adapter_up_weight)
    both_recv = lax.all_to_all(
        jnp.concatenate([down_send, up_send], axis=-1), "dp", split_axis=0, concat_axis=0, tiled=True
    )
    down_recv, up_recv = both_recv[..., :query_width], both_recv[..., query_width:]
    take = (
        (my_owner[:, None, None] == owner_ids[None, :, None])
        & (my_slot[:, None, None] == slot_ids[None, None, :])
    ).astype(jnp.bfloat16)
    down_mine = jnp.einsum(
        "sdc,dcrf->srf", take, down_recv, preferred_element_type=jnp.float32
    ).astype(jnp.bfloat16)
    up_mine = jnp.einsum("sdc,dcro->sro", take, up_recv, preferred_element_type=jnp.float32).astype(
        jnp.bfloat16
    )
    lowrank = rank_total(
        jnp.einsum("sxf,srf->sxr", context_seg, down_mine, preferred_element_type=jnp.float32)
    ).astype(jnp.bfloat16)
    adapter_delta = jnp.einsum(
        "sxr,sro->sxo", lowrank, up_mine, preferred_element_type=jnp.float32
    ).astype(jnp.bfloat16)
    adapter_delta = adapter_delta.reshape(tok_rows, adapter_delta.shape[-1])
    context, adapter_delta = lax.optimization_barrier((context, adapter_delta))
    pieces = []
    for piece, gathered in enumerate(gathered_weights):
        if chained:
            own = output_weight[:, piece * piece_width : (piece + 1) * piece_width]
            summed = chain_project(context, own, gathered)
        else:
            blocks = gathered.reshape(group_count, query_width, piece_width)
            partial_value = jnp.einsum(
                "tf,dfc->tdc", context, blocks, preferred_element_type=jnp.float32
            ).reshape(tok_rows, -1)
            summed = lax.psum_scatter(partial_value, "tensor", scatter_dimension=1, tiled=True)
        pieces.append(summed.reshape(tok_rows, -1, 1, piece_width))
    base_output = jnp.concatenate(pieces, axis=2).reshape(tok_rows, -1)
    projected = base_output + adapter_scale * adapter_delta.astype(jnp.float32)
    return projected.astype(jnp.bfloat16)


def solution(mesh):
    in_specs = (
        P(("parts", "dp"), "tensor"),
        P("parts", "tensor"),
        P("parts", "tensor"),
        P(("parts", "dp"), "tensor"),
        P(("parts", "dp"), "tensor"),
        P("tensor", "dp"),
        P(("parts", "dp"), None, "tensor"),
        P(("parts", "dp"), None, "tensor"),
        P("parts"),
        P("parts"),
        P("parts"),
        P("parts"),
    )
    out_specs = P(("parts", "dp"), "tensor")
    return jax.shard_map(local, mesh=mesh, in_specs=in_specs, out_specs=out_specs, check_vma=False)
```

```python
import jax
import jax.numpy as jnp
from jax import lax
from jax.sharding import PartitionSpec as P

HD = 128
CAP = 1
PIECES = 2


adapter_scale = 2.0


def rank_total(partial_value):
    return lax.psum(partial_value, "tensor")


def local_attention(
    queries, prefix_key_cache, prefix_value_cache, prompt_keys, prompt_values, token_prefix
):
    tok_rows, query_width = queries.shape
    positions, key_width = prefix_key_cache.shape
    local_kv = key_width // HD
    group_size = query_width // key_width
    scale = HD ** (-0.5)
    query_four = queries.reshape(tok_rows, local_kv, group_size, HD)
    cache_keys = prefix_key_cache.reshape(positions, local_kv, HD)
    cache_values = prefix_value_cache.reshape(positions, local_kv, HD)
    own_key_heads = prompt_keys.reshape(tok_rows, local_kv, HD)
    own_value_heads = prompt_values.reshape(tok_rows, local_kv, HD)
    scores = (
        jnp.einsum("tkgd,pkd->kgtp", query_four, cache_keys, preferred_element_type=jnp.float32)
        * scale
    )
    own_score = (
        jnp.einsum("tkgd,tkd->kgt", query_four, own_key_heads, preferred_element_type=jnp.float32)
        * scale
    )
    valid = jnp.arange(positions, dtype=jnp.int32)[None, :] < token_prefix[:, None]
    scores = jnp.where(valid[None, None], scores, -jnp.inf)
    highest = jnp.maximum(jnp.max(scores, axis=-1), own_score)
    expon = jnp.exp(scores - highest[..., None])
    own_expon = jnp.exp(own_score - highest)
    total = jnp.sum(expon, axis=-1) + own_expon
    weights = (expon / total[..., None]).astype(jnp.bfloat16)
    own_weight = (own_expon / total).astype(jnp.bfloat16)
    context = jnp.einsum(
        "kgtp,pkd->tkgd", weights, cache_values, preferred_element_type=jnp.float32
    )
    context = context + jnp.einsum(
        "kgt,tkd->tkgd", own_weight, own_value_heads, preferred_element_type=jnp.float32
    )
    return context.reshape(tok_rows, query_width).astype(jnp.bfloat16)


def selected_blocks(local_adapter_index, adapter_down_weight, adapter_up_weight):
    adapter_number = adapter_down_weight.shape[0]
    adapter_selector = (
        local_adapter_index[..., None] == jnp.arange(adapter_number, dtype=jnp.int32)
    ).astype(jnp.bfloat16)
    down_selected = jnp.einsum(
        "ljm,mes->ljes", adapter_selector, adapter_down_weight, preferred_element_type=jnp.float32
    ).astype(jnp.bfloat16)
    up_selected = jnp.einsum(
        "yuv,vzj->yuzj", adapter_selector, adapter_up_weight, preferred_element_type=jnp.float32
    ).astype(jnp.bfloat16)
    return (down_selected, up_selected)


def chain_gather(pieces_in, units):
    group = lax.axis_index("dp")
    up = [(0, 1), (1, 2), (2, 3)]
    down = [(1, 0), (2, 1), (3, 2)]
    swap = [(0, 1), (1, 0)]
    count = len(pieces_in)
    units = list(units)
    from_low = [lax.ppermute(piece, "dp", up) for piece in pieces_in]
    from_high = [lax.ppermute(piece, "dp", down) for piece in pieces_in]
    first_high = list(from_high)
    slots = [[] for _ in range(count)]
    next_unit = 2
    for step in range(1, 4):
        for piece in range(count):
            low, high = lax.optimization_barrier((from_low[piece], from_high[piece]))
            if step == 1:
                first_high[piece] = high
                mine = jnp.where(group >= 1, low, high)
            elif step == 2:
                mine = jnp.where(group >= 2, low, high)
            else:
                mine = jnp.where(
                    group == 3, low, jnp.where(group == 0, high, first_high[piece])
                )
            if step > 1:
                before, other = slots[piece][-1]
                mine, low, high, other = lax.optimization_barrier((mine, low, high, other))
                slots[piece][-1] = (before, other)
            else:
                mine, low, high = lax.optimization_barrier((mine, low, high))
            if next_unit < len(units) and step > 1 and piece == 0:
                units[next_unit], mine, low, high = lax.optimization_barrier(
                    (units[next_unit], mine, low, high)
                )
                next_unit += 1
            slots[piece].append((mine, lax.ppermute(mine, "parts", swap)))
            if step < 3:
                from_low[piece] = lax.ppermute(low, "dp", up)
                from_high[piece] = lax.ppermute(high, "dp", down)
    return slots, units


def chain_project(context, own, slots):
    group = lax.axis_index("dp")
    part = lax.axis_index("parts")
    tensor = lax.axis_index("tensor")
    core, chip = tensor % 2, tensor // 2
    half = own.shape[0] // 2
    context_mine = lax.dynamic_slice_in_dim(context, part * half, half, axis=1)
    context_other = lax.dynamic_slice_in_dim(context, (1 - part) * half, half, axis=1)
    results = [jnp.dot(context, own, preferred_element_type=jnp.float32).astype(jnp.bfloat16)]
    for mine, other in slots:
        value = jnp.dot(context_mine, mine, preferred_element_type=jnp.float32)
        value = value + jnp.dot(context_other, other, preferred_element_type=jnp.float32)
        results.append(value.astype(jnp.bfloat16))
    stack = jnp.stack(results)
    first = jnp.where(group >= 1, group - 1, 1)
    second = jnp.where(group >= 2, group - 2, group + 2)
    third = jnp.where(group == 3, 0, jnp.where(group == 0, 3, group + 1))
    order = jnp.stack([group, first, second, third])

    def block(index):
        slot = jnp.sum(jnp.where(order == index, jnp.arange(4, dtype=jnp.int32), 0))
        return lax.dynamic_index_in_dim(stack, slot, 0, keepdims=False)

    core_swap = [(0, 1), (1, 0), (2, 3), (3, 2)]
    chip_swap = [(0, 2), (2, 0), (1, 3), (3, 1)]
    far = jnp.stack([block(1 - core), block(3 - core)])
    far = lax.ppermute(far, "tensor", core_swap).astype(jnp.float32)
    near = jnp.stack([block(core), block(2 + core)]).astype(jnp.float32) + far
    sent = lax.dynamic_index_in_dim(near, 1 - chip, 0, keepdims=False).astype(jnp.bfloat16)
    kept = lax.dynamic_index_in_dim(near, chip, 0, keepdims=False)
    return kept + lax.ppermute(sent, "tensor", chip_swap).astype(jnp.float32)


def local(
    queries,
    prefix_key_cache,
    prefix_value_cache,
    prompt_keys,
    prompt_values,
    output_weight,
    adapter_down_weight,
    adapter_up_weight,
    adapter_row_map,
    prompt_adapter,
    prompt_length,
    prefix_read_length,
):
    group_count = lax.axis_size("dp")
    group = lax.axis_index("dp")
    tok_rows, query_width = queries.shape
    part_count = lax.axis_size("parts")
    half_rows = query_width // part_count
    piece_width = output_weight.shape[1] // PIECES
    half_weight = lax.dynamic_slice_in_dim(
        output_weight, lax.axis_index("parts") * half_rows, half_rows, axis=0
    )
    pieces_in = [
        half_weight[:, piece * piece_width : (piece + 1) * piece_width] for piece in range(PIECES)
    ]
    chained = group_count == 4 and part_count == 2 and lax.axis_size("tensor") == 4
    prompt_count = prompt_length.shape[0] // group_count
    seg_rows = tok_rows // prompt_count
    first_prompt = group * prompt_count
    my_lengths = lax.dynamic_slice_in_dim(prompt_length, first_prompt, prompt_count)
    my_prefix = lax.dynamic_slice_in_dim(prefix_read_length, first_prompt, prompt_count)
    token_prefix = jnp.repeat(my_prefix, seg_rows, total_repeat_length=tok_rows)
    if chained:
        local_kv = prefix_key_cache.shape[1] // HD
        heads_width = query_width // local_kv
        units = []
        for prompt in range(prompt_count):
            rows = slice(prompt * seg_rows, (prompt + 1) * seg_rows)
            for head in range(local_kv):
                columns = slice(head * HD, (head + 1) * HD)
                units.append(
                    (
                        queries[rows, head * heads_width : (head + 1) * heads_width],
                        prefix_key_cache[:, columns],
                        prefix_value_cache[:, columns],
                        prompt_keys[rows, columns],
                        prompt_values[rows, columns],
                        token_prefix[rows],
                    )
                )
        gathered_weights, units = chain_gather(pieces_in, units)
        outs = [local_attention(*unit) for unit in units]
        context = jnp.concatenate(
            [
                jnp.concatenate(outs[prompt * local_kv : (prompt + 1) * local_kv], axis=1)
                for prompt in range(prompt_count)
            ],
            axis=0,
        )
    else:
        gathered_weights = [lax.all_gather(piece, ("dp", "parts"), axis=0) for piece in pieces_in]
        context = local_attention(
            queries, prefix_key_cache, prefix_value_cache, prompt_keys, prompt_values, token_prefix
        )
    token_length = jnp.repeat(my_lengths, seg_rows, total_repeat_length=tok_rows)
    live_rows = jnp.arange(tok_rows, dtype=jnp.int32) % seg_rows < token_length
    context = context * live_rows.astype(jnp.bfloat16)[:, None]
    adapter_count = adapter_row_map.shape[0]
    adapter_local_row = adapter_down_weight.shape[0]
    matches = prompt_adapter[:, None] == jnp.arange(adapter_count, dtype=jnp.int32)[None, :]
    stored_all = jnp.sum(jnp.where(matches, adapter_row_map[None, :], 0), axis=1)
    owners = (stored_all // adapter_local_row).reshape(group_count, prompt_count)
    local_rows = (stored_all % adapter_local_row).reshape(group_count, prompt_count)
    same_owner = owners[:, :, None] == owners[:, None, :]
    earlier = jnp.arange(prompt_count)[None, None, :] < jnp.arange(prompt_count)[None, :, None]
    slots = jnp.sum(same_owner & earlier, axis=2)
    my_owner = lax.dynamic_index_in_dim(owners, group, 0, keepdims=False)
    my_slot = lax.dynamic_index_in_dim(slots, group, 0, keepdims=False)
    context_seg = context.reshape(prompt_count, seg_rows, query_width)
    owner_ids = jnp.arange(group_count, dtype=jnp.int32)
    slot_ids = jnp.arange(CAP, dtype=jnp.int32)
    give_mask = (owners == group)[:, None, :] & (slots[:, None, :] == slot_ids[None, :, None])
    which_give = jnp.sum(jnp.where(give_mask, local_rows[:, None, :], 0), axis=2)
    down_send, up_send = selected_blocks(which_give, adapter_down_weight, adapter_up_weight)
    both_recv = lax.all_to_all(
        jnp.concatenate([down_send, up_send], axis=-1), "dp", split_axis=0, concat_axis=0, tiled=True
    )
    down_recv, up_recv = both_recv[..., :query_width], both_recv[..., query_width:]
    take = (
        (my_owner[:, None, None] == owner_ids[None, :, None])
        & (my_slot[:, None, None] == slot_ids[None, None, :])
    ).astype(jnp.bfloat16)
    down_mine = jnp.einsum(
        "sdc,dcrf->srf", take, down_recv, preferred_element_type=jnp.float32
    ).astype(jnp.bfloat16)
    up_mine = jnp.einsum("sdc,dcro->sro", take, up_recv, preferred_element_type=jnp.float32).astype(
        jnp.bfloat16
    )
    lowrank = rank_total(
        jnp.einsum("sxf,srf->sxr", context_seg, down_mine, preferred_element_type=jnp.float32)
    ).astype(jnp.bfloat16)
    adapter_delta = jnp.einsum(
        "sxr,sro->sxo", lowrank, up_mine, preferred_element_type=jnp.float32
    ).astype(jnp.bfloat16)
    adapter_delta = adapter_delta.reshape(tok_rows, adapter_delta.shape[-1])
    context, adapter_delta = lax.optimization_barrier((context, adapter_delta))
    pieces = []
    for piece, gathered in enumerate(gathered_weights):
        if chained:
            own = output_weight[:, piece * piece_width : (piece + 1) * piece_width]
            summed = chain_project(context, own, gathered)
        else:
            blocks = gathered.reshape(group_count, query_width, piece_width)
            partial_value = jnp.einsum(
                "tf,dfc->tdc", context, blocks, preferred_element_type=jnp.float32
            ).reshape(tok_rows, -1)
            summed = lax.psum_scatter(partial_value, "tensor", scatter_dimension=1, tiled=True)
        pieces.append(summed.reshape(tok_rows, -1, 1, piece_width))
    base_output = jnp.concatenate(pieces, axis=2).reshape(tok_rows, -1)
    projected = base_output + adapter_scale * adapter_delta.astype(jnp.float32)
    return projected.astype(jnp.bfloat16)


def solution(mesh):
    in_specs = (
        P(("parts", "dp"), "tensor"),
        P("parts", "tensor"),
        P("parts", "tensor"),
        P(("parts", "dp"), "tensor"),
        P(("parts", "dp"), "tensor"),
        P("tensor", "dp"),
        P(("parts", "dp"), None, "tensor"),
        P(("parts", "dp"), None, "tensor"),
        P("parts"),
        P("parts"),
        P("parts"),
        P("parts"),
    )
    out_specs = P(("parts", "dp"), "tensor")
    return jax.shard_map(local, mesh=mesh, in_specs=in_specs, out_specs=out_specs, check_vma=False)
```
